32 devices in a mesh: expert: 4 (over y, x), req: 8 (over z, core).
Axes of the slice: x: 2, y: 2, z: 4, core: 2. Of those that a mesh axis runs over, the one named last changes fastest.
Arguments:
- queries: bfloat16 [8192, 1024], P(('expert', 'req')), may hold values from -82 to 82
- self_kv: bfloat16 [8192, 2048], P(('expert', 'req')), may hold values from -4 to 4
- kv_pages: bfloat16 [32, 128, 2048], P(('expert', 'req')), may hold values from -4 to 4
- page_table: int32 [4, 8], P('expert'), may hold values from 0 to 7, as said below
- lengths: int32 [8192], P(('expert', 'req')), may hold values from 1 to 1024
- routes: int32 [8192, 2], P(('expert', 'req')), may hold values from 0 to 3, all different within a row
- residual: bfloat16 [8192, 1024], P(('expert', 'req')), may hold values from -20 to 20
- w_attn_out: bfloat16 [1024, 1024], replicated, may hold values from -0.1875 to 0.1875
- gain_attn: bfloat16 [1024], replicated, may hold values from 0.25 to 1.75
- w_router: bfloat16 [1024, 4], replicated, may hold values from -0.1875 to 0.1875
- w_in: bfloat16 [4, 1024, 2816], P('expert'), may hold values from -0.1875 to 0.1875
- w_out: bfloat16 [4, 1408, 1024], P('expert'), may hold values from -0.15625 to 0.15625
- gain_out: bfloat16 [1024], replicated, may hold values from 0.25 to 1.75
Outputs:
- layer_out: bfloat16 [8192, 1024], P(('expert', 'req'))
The draws below stay inside these ranges and needn't reach their ends.
Inputs may be any that keep to these rules, and one draw needn't show every extreme that they name: Each row of page_table is a permutation of 0 to 7.
All inputs are finite; a program needn't handle non-finite values.
Results may differ from the reference program's by a relative error of at most 0.01.
Values may be sent and summed in bfloat16 or wider, within the bound.
A program may use at most 128 MiB of HBM per device.

```python
import math
from functools import partial
import jax
import jax.numpy as jnp
from jax import lax

D = 1024
HEADS = 16
HEAD_DIM = 64
FFW = 1408
TOP = 2
PAGE = 128
ROWS_DEV = 256
HD = 1024
EXPERTS = 4
CAP = 160
GROUPS = 4
ROWS_GRP = 2048
TOKENS = 8192
GROUP_PAGES = 8
CTX = 1024
PAGES_ALL = 32
DEVICES = 32


def permute_one(subkey):
    return jax.random.permutation(subkey, GROUP_PAGES)


def table_draw(base_key):
    subkeys = jax.random.split(jax.random.fold_in(base_key, 101), GROUPS)
    return jax.vmap(permute_one)(subkeys).astype(jnp.int32)


def pages_draw(base_key):
    subkey = jax.random.fold_in(base_key, 202)
    array_shape = (PAGES_ALL, PAGE, 2 * HD)
    return jnp.clip(jax.random.normal(subkey, array_shape, jnp.float32), -4.0, 4.0)


def draw_queries(key, part):
    subkey = jax.random.fold_in(key, 303)
    return jnp.clip(jax.random.normal(subkey, (TOKENS, HD), jnp.float32), -4.0, 4.0).astype(jnp.bfloat16)


def draw_self_kv(key, part):
    subkey = jax.random.fold_in(key, 404)
    return jnp.clip(jax.random.normal(subkey, (TOKENS, 2 * HD), jnp.float32), -4.0, 4.0).astype(jnp.bfloat16)


def draw_kv_pages(key, part):
    return pages_draw(key).astype(jnp.bfloat16)


def draw_page_table(key, part):
    return table_draw(key)


def draw_lengths(key, part):
    values = jax.random.randint(jax.random.fold_in(key, 505), (TOKENS,), 1, CTX + 1, dtype=jnp.int32)
    row_index = jnp.arange(TOKENS, dtype=jnp.int32)
    return jnp.where(row_index % ROWS_GRP == 0, CTX, values).astype(jnp.int32)


def draw_residual(key, part):
    row_scale = jnp.exp(jax.random.uniform(jax.random.fold_in(key, 606), (TOKENS, 1), jnp.float32, -1.15, 1.15))
    col_scale = jnp.exp(jax.random.uniform(jax.random.fold_in(key, 607), (1, D), jnp.float32, -1.15, 1.15))
    base_rows = 0.5 * jnp.clip(jax.random.normal(jax.random.fold_in(key, 609), (TOKENS, D), jnp.float32), -4.0, 4.0)
    return (base_rows * row_scale * col_scale).astype(jnp.bfloat16)


def block_levels(stream_key, shape, cuts, low, top_value):
    def one(axis_at, blocks):
        draws = jax.random.uniform(jax.random.fold_in(jax.random.fold_in(stream_key, 6), axis_at), (blocks,), jnp.float32, low / len(cuts), top_value / len(cuts))
        return jnp.repeat(jnp.exp(draws), shape[axis_at] // blocks).reshape((-1,) + (1,) * (len(shape) - axis_at - 1))

    factor_of = one(*cuts[0])
    for cut in cuts[1:]:
        factor_of = factor_of * one(*cut)
    return factor_of


def picks_of(rng, rows, count, top, lift):
    sequence = jax.random.permutation(jax.random.fold_in(rng, 1), count)
    favour = sequence
    for power in range(3):
        favour = favour * favour // count
    favour = favour * lift // count
    lots = jax.random.randint(jax.random.fold_in(rng, 2), (rows, count), 0, 4096) + favour
    fixed_rows = jax.random.permutation(jax.random.fold_in(rng, 3), rows)[jnp.arange(count) % rows]
    lots = jnp.where(jnp.arange(rows)[:, None] == fixed_rows[None, :], 1 << 14, lots)
    score = lots * count + jnp.arange(count)
    return lax.top_k(score.astype(jnp.int32), top)[1].astype(jnp.int32)


def noise(rng, shape, spread, most, shards=(), kind=jnp.bfloat16):
    entries = spread * jax.random.normal(rng, shape, jnp.float32)
    if shards:
        entries = entries * block_levels(rng, shape, shards, -0.22, 0.18)
    return jnp.clip(entries, -most, most).astype(kind)


def setup_inputs(seed: int = 0) -> dict:
    key_of = jax.random.split(jax.random.key(seed), 14)
    queries = draw_queries(jax.random.fold_in(key_of[13], 71), 0)
    self_kv = draw_self_kv(jax.random.fold_in(key_of[13], 71), 0)
    kv_pages = draw_kv_pages(jax.random.fold_in(key_of[13], 71), 0)
    page_table = draw_page_table(jax.random.fold_in(key_of[13], 71), 0)
    lengths = draw_lengths(jax.random.fold_in(key_of[13], 71), 0)
    routes = picks_of(key_of[5], TOKENS, EXPERTS, TOP, 8192)
    residual = draw_residual(jax.random.fold_in(key_of[13], 71), 0)
    w_attn_out = noise(key_of[7], (HD, D), HD ** -0.5, 0.1875)
    gain_attn = jnp.clip(1.0 + 0.15 * jax.random.normal(key_of[8], (D,), jnp.float32), 0.25, 1.75).astype(jnp.bfloat16)
    w_router = noise(key_of[9], (D, EXPERTS), D ** -0.5, 0.1875)
    w_in = noise(key_of[10], (EXPERTS, D, 2 * FFW), D ** -0.5, 0.1875, ((0, 4),))
    w_out = noise(key_of[11], (EXPERTS, FFW, D), FFW ** -0.5, 0.15625, ((0, 4),))
    gain_out = jnp.clip(1.0 + 0.15 * jax.random.normal(key_of[12], (D,), jnp.float32), 0.25, 1.75).astype(jnp.bfloat16)
    return dict(queries=queries, self_kv=self_kv, kv_pages=kv_pages, page_table=page_table, lengths=lengths, routes=routes, residual=residual, w_attn_out=w_attn_out, gain_attn=gain_attn, w_router=w_router, w_in=w_in, w_out=w_out, gain_out=gain_out)


norm_eps = 1e-06

def key_positions(table_row, first_index, key_count, page_len):
    logical = jnp.arange(table_row.shape[0], dtype=jnp.int32)
    inverse = lax.optimization_barrier(jnp.sum(jnp.where(table_row[:, None] == logical[None, :], logical[:, None], 0), axis=0)).astype(jnp.int32)
    flat_index = first_index + jnp.arange(key_count, dtype=jnp.int32)
    page_index = flat_index // page_len
    logical_page = lax.optimization_barrier(jnp.sum(jnp.where(page_index[:, None] == logical[None, :], inverse[None, :], 0), axis=1)).astype(jnp.int32)
    return logical_page * page_len + flat_index % page_len

def rms_scale(values, gain_row):
    mean_square = lax.optimization_barrier(jnp.mean(values * values, axis=-1, keepdims=True))
    return values * lax.rsqrt(mean_square + norm_eps) * gain_row.astype(jnp.float32)

def head_attention(query_h, own_key, own_value, key_h, value_h, visible):
    scale_qk = 1.0 / math.sqrt(HEAD_DIM)
    scores = jnp.dot(query_h, key_h.T, preferred_element_type=jnp.float32) * scale_qk
    own_score = lax.optimization_barrier(jnp.sum(query_h.astype(jnp.float32) * own_key.astype(jnp.float32), axis=1)) * scale_qk
    masked = jnp.where(visible, scores, -jnp.inf)
    highest = jnp.maximum(lax.optimization_barrier(jnp.max(masked, axis=1)), own_score)
    weights = jnp.exp(masked - highest[:, None])
    own_weight = jnp.exp(own_score - highest)
    weight_sum = own_weight + lax.optimization_barrier(jnp.sum(weights, axis=1))
    own_rounded = lax.optimization_barrier(own_weight.astype(jnp.bfloat16))
    weighted = jnp.dot(weights.astype(jnp.bfloat16), value_h, preferred_element_type=jnp.float32)
    weighted = weighted + own_rounded.astype(jnp.float32)[:, None] * own_value.astype(jnp.float32)
    return weighted / weight_sum[:, None]

def group_attention(group_inputs):
    query_g, selfkv_g, pages_g, table_row, length_g = group_inputs
    rows_g = query_g.shape[0]
    positions = key_positions(table_row, 0, pages_g.shape[0], PAGE)
    visible = positions[None, :] < length_g[:, None]
    query_h = query_g.reshape(rows_g, HEADS, HEAD_DIM).transpose(1, 0, 2)
    own_keys = selfkv_g[:, :HD].reshape(rows_g, HEADS, HEAD_DIM).transpose(1, 0, 2)
    own_values = selfkv_g[:, HD:].reshape(rows_g, HEADS, HEAD_DIM).transpose(1, 0, 2)
    key_h = pages_g[:, :HD].reshape(-1, HEADS, HEAD_DIM).transpose(1, 0, 2)
    value_h = pages_g[:, HD:].reshape(-1, HEADS, HEAD_DIM).transpose(1, 0, 2)

    def one_head(head_inputs):
        return head_attention(head_inputs[0], head_inputs[1], head_inputs[2], head_inputs[3], head_inputs[4], visible)
    result = lax.map(one_head, (query_h, own_keys, own_values, key_h, value_h))
    return result.transpose(1, 0, 2).reshape(rows_g, HD).astype(jnp.bfloat16)

def route_block(route_rows, cap_size, expert_count):
    onehot = (route_rows[:, :, None] == jnp.arange(expert_count, dtype=jnp.int32)[None, None, :]).astype(jnp.int32)
    ordered = onehot.transpose(1, 0, 2).reshape(-1, expert_count)
    earlier = (jnp.cumsum(ordered, axis=0) - ordered).astype(jnp.int32)
    position = lax.optimization_barrier(jnp.sum(earlier * ordered, axis=1)).astype(jnp.int32).reshape(route_rows.shape[1], route_rows.shape[0])
    kept_mask = position < cap_size
    slot_ids = jnp.where(kept_mask, route_rows.T * cap_size + position, -1).astype(jnp.int32)
    return (onehot, kept_mask, slot_ids)

def take_rows(table_rows, index_rows):
    return table_rows[index_rows]

def reference(queries, self_kv, kv_pages, page_table, lengths, routes, residual, w_attn_out, gain_attn, w_router, w_in, w_out, gain_out):
    attended = lax.map(group_attention, (queries.reshape(GROUPS, ROWS_GRP, HD), self_kv.reshape(GROUPS, ROWS_GRP, 2 * HD), kv_pages.reshape(GROUPS, GROUP_PAGES * PAGE, 2 * HD), page_table, lengths.reshape(GROUPS, ROWS_GRP))).reshape(TOKENS, HD)
    residual_sum = residual.astype(jnp.float32) + jnp.dot(attended, w_attn_out, preferred_element_type=jnp.float32)
    normed = rms_scale(residual_sum, gain_attn).astype(jnp.bfloat16)
    logits = jnp.dot(normed, w_router, preferred_element_type=jnp.float32)
    onehot, kept_mask, slot_ids = jax.vmap(partial(route_block, cap_size=CAP, expert_count=EXPERTS))(routes.reshape(DEVICES, ROWS_DEV, TOP))
    slot_range = jnp.arange(EXPERTS * CAP, dtype=jnp.int32)
    assign = lax.optimization_barrier(jnp.sum((slot_ids[:, :, None, :] == slot_range[None, None, :, None]).astype(jnp.float32), axis=1))
    normed_dev = normed.reshape(DEVICES, ROWS_DEV, D)
    buffer = jnp.einsum('dsr,drc->dsc', assign, normed_dev.astype(jnp.float32)).astype(jnp.bfloat16)
    by_expert = buffer.reshape(DEVICES, EXPERTS, CAP, D).transpose(1, 0, 2, 3).reshape(EXPERTS, DEVICES * CAP, D)

    def one_expert(expert_inputs):
        rows_e, gate_up, down_proj = expert_inputs
        inner_act = jnp.dot(rows_e, gate_up, preferred_element_type=jnp.float32)
        hidden = (jax.nn.gelu(inner_act[:, :FFW], approximate=True) * inner_act[:, FFW:]).astype(jnp.bfloat16)
        return jnp.dot(hidden, down_proj, preferred_element_type=jnp.float32).astype(jnp.bfloat16)
    outcome = lax.map(one_expert, (by_expert, w_in, w_out))
    outcome = outcome.reshape(EXPERTS, DEVICES, CAP, D).transpose(1, 0, 2, 3).reshape(DEVICES, EXPERTS * CAP, D)
    picked_rows = jax.vmap(take_rows)(outcome, jnp.maximum(slot_ids, 0))
    logits_dev = logits.reshape(DEVICES, ROWS_DEV, EXPERTS)
    picked = lax.optimization_barrier(jnp.sum(jnp.where(onehot > 0, logits_dev[:, :, None, :], 0.0), axis=3))
    gate_values = jax.nn.sigmoid(picked - picked[:, :, ::-1])
    gate_kept = jnp.where(kept_mask, gate_values.transpose(0, 2, 1), 0.0)
    mixture = lax.optimization_barrier(jnp.sum(picked_rows.astype(jnp.float32) * gate_kept[..., None], axis=1)).reshape(TOKENS, D)
    return rms_scale(residual_sum + mixture, gain_out).astype(jnp.bfloat16)
```

```python
import math

import jax
import jax.numpy as jnp
from jax import lax
from jax.sharding import PartitionSpec as P

HEADS = 16
HEAD_DIM = 64
TOP = 2
PAGE = 128
HD = 1024


norm_eps = 1e-06


def block_size(total_count, largest):
    chosen = min(total_count, largest)
    while total_count % chosen:
        chosen -= 1
    return chosen


def key_positions(table_row, key_count, page_len):
    logical = jnp.arange(table_row.shape[0], dtype=jnp.int32)
    inverse = jnp.sum(
        jnp.where(table_row[:, None] == logical[None, :], logical[:, None], 0), axis=0
    )
    flat_index = jnp.arange(key_count, dtype=jnp.int32)
    page_index = flat_index // page_len
    logical_page = jnp.sum(
        jnp.where(page_index[:, None] == logical[None, :], inverse[None, :], 0), axis=1
    )
    return logical_page * page_len + flat_index % page_len


def rms_scale(values, gain_row):
    mean_square = jnp.mean(values * values, axis=-1, keepdims=True)
    return values * lax.rsqrt(mean_square + norm_eps) * gain_row.astype(jnp.float32)


def route_block(route_rows, cap_size, expert_count):
    onehot = (
        route_rows[:, :, None] == jnp.arange(expert_count, dtype=jnp.int32)[None, None, :]
    ).astype(jnp.int32)
    ordered = onehot.transpose(1, 0, 2).reshape(-1, expert_count)
    total = ordered.shape[0]
    before = jnp.arange(total)[:, None] > jnp.arange(total)[None, :]
    earlier = jnp.dot(
        before.astype(jnp.bfloat16),
        ordered.astype(jnp.bfloat16),
        preferred_element_type=jnp.float32,
    ).astype(jnp.int32)
    position = jnp.sum(earlier * ordered, axis=1).reshape(route_rows.shape[1], route_rows.shape[0])
    kept_mask = position < cap_size
    slot_ids = jnp.where(kept_mask, route_rows.T * cap_size + position, -1)
    return (onehot, kept_mask, slot_ids)


def on_device(
    queries,
    self_kv,
    kv_pages,
    page_table,
    lengths,
    routes,
    residual,
    w_attn_out,
    gain_attn,
    w_router,
    w_in,
    w_out,
    gain_out,
):
    row_count = queries.shape[0]
    scale_qk = 1.0 / math.sqrt(HEAD_DIM)
    table_row = page_table[0]
    page_rows = kv_pages.reshape(-1, kv_pages.shape[-1])
    query_h = queries.reshape(row_count, HEADS, HEAD_DIM)
    own_key = self_kv[:, :HD].reshape(row_count, HEADS, HEAD_DIM)
    own_value = self_kv[:, HD:].reshape(row_count, HEADS, HEAD_DIM)
    own_score = (
        jnp.einsum("rhd,rhd->hr", query_h, own_key, preferred_element_type=jnp.float32) * scale_qk
    )
    start_value = jnp.swapaxes(own_value, 0, 1).astype(jnp.float32)
    initial = (own_score, jnp.ones_like(own_score), start_value)
    page_piece = lax.all_gather(page_rows, "req", axis=0, tiled=True)
    piece_len = page_piece.shape[0]
    step_len = block_size(piece_len, 512)
    positions = key_positions(table_row, piece_len, PAGE)
    blocks = page_piece.reshape(piece_len // step_len, step_len, page_piece.shape[1])
    block_pos = positions.reshape(piece_len // step_len, step_len)

    def add_block(running, block_items):
        highest, weight_sum, weighted = running
        block_rows, block_place = block_items
        key_rows = block_rows[:, :HD].reshape(step_len, HEADS, HEAD_DIM)
        value_rows = block_rows[:, HD:].reshape(step_len, HEADS, HEAD_DIM)
        scores = (
            jnp.einsum("rhd,khd->hrk", query_h, key_rows, preferred_element_type=jnp.float32)
            * scale_qk
        )
        visible = block_place[None, :] < lengths[:, None]
        masked = jnp.where(visible[None], scores, -jnp.inf)
        new_high = jnp.maximum(highest, jnp.max(masked, axis=2))
        factor = jnp.exp(highest - new_high)
        weights = jnp.exp(masked - new_high[:, :, None])
        weight_sum = weight_sum * factor + jnp.sum(weights, axis=2)
        weighted = weighted * factor[:, :, None] + jnp.einsum(
            "hrk,khd->hrd",
            weights.astype(jnp.bfloat16),
            value_rows,
            preferred_element_type=jnp.float32,
        )
        return ((new_high, weight_sum, weighted), None)

    result, unused = lax.scan(add_block, initial, (blocks, block_pos))
    highest, weight_sum, weighted = result
    attended = (
        (weighted / weight_sum[:, :, None])
        .transpose(1, 0, 2)
        .reshape(row_count, HD)
        .astype(jnp.bfloat16)
    )
    residual_sum = residual.astype(jnp.float32) + jnp.dot(
        attended, w_attn_out, preferred_element_type=jnp.float32
    )
    normed = rms_scale(residual_sum, gain_attn).astype(jnp.bfloat16)
    logits = jnp.dot(normed, w_router, preferred_element_type=jnp.float32)
    experts_all = w_router.shape[1]
    cap_size = (5 * row_count * TOP + 4 * experts_all - 1) // (4 * experts_all)
    onehot, kept_mask, slot_ids = route_block(routes, cap_size, experts_all)
    picked = jnp.sum(jnp.where(onehot > 0, logits[:, None, :], 0.0), axis=2)
    gate_values = jax.nn.sigmoid(picked - picked[:, ::-1])
    slot_range = jnp.arange(experts_all * cap_size, dtype=jnp.int32)
    assign = jnp.sum(
        (slot_ids[:, None, :] == slot_range[None, :, None]).astype(jnp.bfloat16), axis=0
    )
    model_width = normed.shape[1]
    buffer = (
        jnp.dot(assign, normed, preferred_element_type=jnp.float32)
        .astype(jnp.bfloat16)
        .reshape(experts_all, cap_size, model_width)
    )
    arrived = lax.all_to_all(buffer, "expert", split_axis=0, concat_axis=0, tiled=True)
    slot_count = arrived.shape[1]
    local_experts = w_in.shape[0]
    hidden_width = w_out.shape[1]
    grouped = arrived.reshape(-1, local_experts, slot_count, model_width)
    inner_act = jnp.einsum("slnd,ldf->slnf", grouped, w_in, preferred_element_type=jnp.float32)
    hidden = (
        jax.nn.gelu(inner_act[..., :hidden_width], approximate=True) * inner_act[..., hidden_width:]
    ).astype(jnp.bfloat16)
    outcome = jnp.einsum(
        "slnf,lfd->slnd", hidden, w_out, preferred_element_type=jnp.float32
    ).astype(jnp.bfloat16)
    expert_done = outcome.reshape(-1, slot_count, model_width)
    collected = lax.all_to_all(expert_done, "expert", split_axis=0, concat_axis=0, tiled=True)
    flat_rows = collected.reshape(-1, model_width)
    picked_rows = flat_rows[jnp.maximum(slot_ids, 0)]
    gate_kept = jnp.where(kept_mask, gate_values.T, 0.0)
    mixture = jnp.sum(picked_rows.astype(jnp.float32) * gate_kept[:, :, None], axis=0)
    return rms_scale(residual_sum + mixture, gain_out).astype(jnp.bfloat16)


def solution(mesh):
    in_specs = (
        P(("expert", "req"), None),
        P(("expert", "req"), None),
        P(("expert", "req"), None, None),
        P("expert", None),
        P(("expert", "req")),
        P(("expert", "req"), None),
        P(("expert", "req"), None),
        P(),
        P(),
        P(),
        P("expert", None, None),
        P("expert", None, None),
        P(),
    )
    out_specs = P(("expert", "req"), None)
    return jax.shard_map(
        on_device, mesh=mesh, in_specs=in_specs, out_specs=out_specs, check_vma=False
    )
```

```python
import functools
import math

import jax
import jax.numpy as jnp
from jax import lax
from jax.experimental import pallas as pl
from jax.experimental.pallas import tpu as pltpu
from jax.sharding import PartitionSpec as P

HEADS = 16
HEAD_DIM = 64
TOP = 2
PAIRS = HEADS // 2
LANES = 2 * HEAD_DIM
HD = HEADS * HEAD_DIM
CORES = 2
HALVES = 2
NORM_EPS = 1e-06
EXP_SCALE = math.log2(math.e) / math.sqrt(HEAD_DIM)
F32 = jnp.float32
BF16 = jnp.bfloat16


def xor_index(a, b, count):
    out, bit = 0, 1
    while bit < count:
        out = out + ((a // bit + b // bit) % 2) * bit
        bit *= 2
    return out


def rms_scale(values, gain_row):
    mean_square = jnp.mean(values * values, axis=-1, keepdims=True)
    return values * lax.rsqrt(mean_square + NORM_EPS) * gain_row


def layer_kernel(
    n_exp,
    n_req,
    q_hbm,
    self_hbm,
    page_hbm,
    table_ref,
    lengths_ref,
    routes_ref,
    routes_t_ref,
    resid_hbm,
    w_attn_hbm,
    gain_attn_ref,
    w_router_ref,
    w_in_hbm,
    w_out_hbm,
    gain_out_ref,
    out_ref,
    kv,
    q,
    self_kv,
    resid_in,
    w_attn,
    w_in,
    w_out,
    bias,
    top,
    acc,
    attended,
    resid,
    normed,
    assign,
    pick,
    gates,
    disp,
    arrived,
    hidden,
    result,
    collected,
    load_sem,
    ring_send,
    pair_send,
    page_recv,
    disp_send,
    disp_recv,
    back_send,
    back_recv,
):
    me_exp = lax.axis_index("expert")
    me_req = lax.axis_index("req")
    z, core = me_req // CORES, me_req % CORES
    n_z = n_req // CORES
    rows = q.shape[0]
    page_len = kv.shape[1]
    half_len = page_len // HALVES
    cap = disp.shape[1]
    hidden_width = w_out.shape[0]
    width = resid.shape[1]
    sibling = z * CORES + (1 - core)

    def at_req(req):
        return {"req": req}

    def at_exp(exp):
        return {"expert": exp}

    loads = [
        (page_hbm.at[0], kv.at[me_req]),
        (q_hbm, q),
        (self_hbm, self_kv),
        (resid_hbm, resid_in),
        (w_attn_hbm, w_attn),
        (w_in_hbm.at[0], w_in),
        (w_out_hbm.at[0], w_out),
    ]
    load = [
        pltpu.make_async_copy(src, dst, load_sem.at[i]) for i, (src, dst) in enumerate(loads)
    ]
    for copy in load:
        copy.start()

    barrier = pltpu.get_barrier_semaphore()

    def greet(device):
        pl.semaphore_signal(
            barrier, inc=1, device_id=device, device_id_type=pl.DeviceIdType.MESH
        )

    greet(at_req(sibling))

    @pl.when(z > 0)
    def _():
        greet(at_req(me_req - CORES))

    @pl.when(z < n_z - 1)
    def _():
        greet(at_req(me_req + CORES))

    for d in range(1, n_exp):
        greet(at_exp(xor_index(me_exp, d, n_exp)))
    pl.semaphore_wait(barrier, n_exp + jnp.where(z > 0, 1, 0) + jnp.where(z < n_z - 1, 1, 0))

    def half_of(page, half):
        return kv.at[page, pl.ds(half * half_len, half_len)]

    def ring_copy(page, half, side, own=False):
        src = page_hbm.at[0, pl.ds(half * half_len, half_len)] if own else half_of(page, half)
        return pltpu.make_async_remote_copy(
            src_ref=src,
            dst_ref=half_of(page, half),
            send_sem=ring_send.at[side, page, half],
            recv_sem=page_recv.at[page, half],
            device_id=at_req(me_req + CORES * (1 - 2 * side)),
            device_id_type=pl.DeviceIdType.MESH,
        )

    def pair_copy(page, half, own=False):
        src = page_hbm.at[0, pl.ds(half * half_len, half_len)] if own else half_of(page, half)
        return pltpu.make_async_remote_copy(
            src_ref=src,
            dst_ref=half_of(page, half),
            send_sem=pair_send.at[page, half],
            recv_sem=page_recv.at[page, half],
            device_id=at_req(sibling),
            device_id_type=pl.DeviceIdType.MESH,
        )

    for half in range(HALVES):

        @pl.when(z < n_z - 1)
        def _():
            ring_copy(me_req, half, 0, own=True).start()

        @pl.when(z > 0)
        def _():
            ring_copy(me_req, half, 1, own=True).start()

    for half in range(HALVES):
        pair_copy(me_req, half, own=True).start()

    strict = (
        lax.broadcasted_iota(jnp.int32, (rows, rows), 0)
        > lax.broadcasted_iota(jnp.int32, (rows, rows), 1)
    ).astype(F32).astype(BF16)
    strict_t = (
        lax.broadcasted_iota(jnp.int32, (rows, rows), 0)
        < lax.broadcasted_iota(jnp.int32, (rows, rows), 1)
    ).astype(F32).astype(BF16)
    exp_lane = lax.broadcasted_iota(jnp.int32, (rows, 128), 1)
    exp_row = lax.broadcasted_iota(jnp.int32, (n_exp, rows), 0)
    total = jnp.zeros((1, 128), F32)
    total_t = jnp.zeros((n_exp, 1), F32)
    slots, slots_t = [], []
    for k in range(TOP):
        route = routes_ref[:, k : k + 1]
        hot = (exp_lane == route).astype(F32)
        before = jnp.dot(strict, hot.astype(BF16), preferred_element_type=F32) + total
        place = jnp.sum(before * hot, axis=1, keepdims=True).astype(jnp.int32)
        slots.append(jnp.where(place < cap, route * cap + place, -1))
        total = total + jnp.sum(hot, axis=0, keepdims=True)
        route_t = routes_t_ref[k : k + 1, :]
        hot_t = (exp_row == route_t).astype(F32)
        before_t = jnp.dot(hot_t.astype(BF16), strict_t, preferred_element_type=F32) + total_t
        place_t = jnp.sum(before_t * hot_t, axis=0, keepdims=True).astype(jnp.int32)
        slots_t.append(jnp.where(place_t < cap, route_t * cap + place_t, -1))
        total_t = total_t + jnp.sum(hot_t, axis=1, keepdims=True)

    def fill_tables(e, carry):
        slot_row = lax.broadcasted_iota(jnp.int32, (cap, rows), 0) + e * cap
        taken = (slot_row == slots_t[0]).astype(F32) + (slot_row == slots_t[1]).astype(F32)
        assign[e] = taken.astype(BF16)
        slot_lane = lax.broadcasted_iota(jnp.int32, (rows, cap), 1) + e * cap
        for k in range(TOP):
            pick[e, k * rows : (k + 1) * rows, :] = (
                (slot_lane == slots[k]).astype(F32).astype(BF16)
            )
        return carry

    lax.fori_loop(0, n_exp, fill_tables, 0)

    first_lanes = lax.broadcasted_iota(jnp.int32, (1, LANES), 1) < HEAD_DIM

    def own_part(pair, carry):
        lanes = pl.ds(pl.multiple_of(pair * LANES, LANES), LANES)
        product = q[:, lanes].astype(F32) * self_kv[:, lanes].astype(F32)
        own_value = self_kv[
            :, pl.ds(pl.multiple_of(HD + pair * LANES, LANES), LANES)
        ].astype(F32)
        for i in range(2):
            mine = first_lanes if i == 0 else jnp.logical_not(first_lanes)
            score = jnp.sum(jnp.where(mine, product, 0.0), axis=1, keepdims=True)
            top[2 * pair + i] = jnp.broadcast_to(score, (rows, LANES))
            acc[2 * pair + i] = jnp.where(mine, own_value, 1.0)
        return carry

    load[1].wait()
    load[2].wait()
    lax.fori_loop(0, PAIRS, own_part, 0)

    keys = CORES * page_len
    table = table_ref[...]
    logical = lax.broadcasted_iota(jnp.int32, table.shape, 1)

    def attend(block_z):
        key_lane = lax.broadcasted_iota(jnp.int32, (1, keys), 1)
        place = key_lane % page_len
        for c in range(CORES):
            at = jnp.sum(
                jnp.where(table == block_z * CORES + c, logical, 0), axis=1, keepdims=True
            )
            place = place + jnp.where(key_lane // page_len == c, at * page_len, 0)
        bias[...] = jnp.where(place < lengths_ref[...], 0.0, -jnp.inf)

        def heads(pair, carry):
            lanes = pl.ds(pl.multiple_of(pair * LANES, LANES), LANES)
            value_lanes = pl.ds(pl.multiple_of(HD + pair * LANES, LANES), LANES)
            query = q[:, lanes]
            key = jnp.concatenate(
                [kv[block_z * CORES + c, :, lanes] for c in range(CORES)], axis=0
            )
            value = jnp.concatenate(
                [kv[block_z * CORES + c, :, value_lanes] for c in range(CORES)], axis=0
            )
            for i in range(2):
                mine = first_lanes if i == 0 else jnp.logical_not(first_lanes)
                score = lax.dot_general(
                    jnp.where(mine, query, jnp.zeros_like(query)),
                    key,
                    (((1,), (1,)), ((), ())),
                    preferred_element_type=F32,
                ) + bias[...]
                old = top[2 * pair + i]
                new = jnp.maximum(old, jnp.max(score, axis=1, keepdims=True))
                weight = jnp.exp2(
                    (score - jnp.concatenate([new] * (keys // LANES), axis=1)) * EXP_SCALE
                )
                factor = jnp.exp2((old - new) * EXP_SCALE)
                top[2 * pair + i] = new
                acc[2 * pair + i] = acc[2 * pair + i] * factor + jnp.dot(
                    weight.astype(BF16),
                    jnp.where(mine, value, jnp.ones_like(value)),
                    preferred_element_type=F32,
                )
            return carry

        def heads_two(step, carry):
            heads(2 * step, carry)
            heads(2 * step + 1, carry)
            return carry

        lax.fori_loop(0, PAIRS // 2, heads_two, 0)

    load[0].wait()
    for half in range(HALVES):
        pair_copy(sibling, half).wait_recv()
    attend(z)

    def stage(s, carry):
        for half in range(HALVES):
            for side in range(2):
                block_z = z - s if side == 0 else z + s
                here = block_z >= 0 if side == 0 else block_z < n_z
                onward = z < n_z - 1 if side == 0 else z > 0
                page = block_z * CORES + core

                @pl.when(here)
                def _():
                    ring_copy(page, half, side).wait_recv()

                    @pl.when(onward)
                    def _():
                        ring_copy(page, half, side).start()

                    pair_copy(page, half).start()

        for side in range(2):
            block_z = z - s if side == 0 else z + s
            here = block_z >= 0 if side == 0 else block_z < n_z

            @pl.when(here)
            def _():
                for half in range(HALVES):
                    pair_copy(block_z * CORES + (1 - core), half).wait_recv()
                attend(block_z)

        return carry

    lax.fori_loop(1, n_z, stage, 0)

    for pair in range(PAIRS):
        first, second = acc[2 * pair], acc[2 * pair + 1]
        attended[:, pair * LANES : (pair + 1) * LANES] = jnp.where(
            first_lanes,
            first / first[:, LANES - 1 : LANES],
            second / second[:, 0:1],
        ).astype(BF16)

    load[3].wait()
    load[4].wait()
    step_cols = 256
    for c in range(0, width, step_cols):
        resid[:, c : c + step_cols] = resid_in[:, c : c + step_cols].astype(F32) + jnp.dot(
            attended[...], w_attn[:, c : c + step_cols], preferred_element_type=F32
        )
    normed[...] = rms_scale(resid[...], gain_attn_ref[...].astype(F32)).astype(BF16)

    def disp_copy(exp, source):
        return pltpu.make_async_remote_copy(
            src_ref=disp.at[exp],
            dst_ref=arrived.at[source],
            send_sem=disp_send.at[exp],
            recv_sem=disp_recv.at[source],
            device_id=at_exp(exp),
            device_id_type=pl.DeviceIdType.MESH,
        )

    def back_copy(source, exp):
        return pltpu.make_async_remote_copy(
            src_ref=result.at[source],
            dst_ref=collected.at[exp],
            send_sem=back_send.at[source],
            recv_sem=back_recv.at[exp],
            device_id=at_exp(source),
            device_id_type=pl.DeviceIdType.MESH,
        )

    def gather_slots(exp):
        return jnp.dot(assign[exp], normed[...], preferred_element_type=F32).astype(BF16)

    def send_slots(d, carry):
        exp = xor_index(me_exp, d, n_exp)
        disp[exp] = gather_slots(exp)
        disp_copy(exp, me_exp).start()
        return carry

    lax.fori_loop(1, n_exp, send_slots, 0)
    arrived[me_exp] = gather_slots(me_exp)

    logits = jnp.dot(normed[...], w_router_ref[...], preferred_element_type=F32)
    router_lane = lax.broadcasted_iota(jnp.int32, logits.shape, 1)
    chosen = [
        jnp.sum(
            jnp.where(router_lane == routes_ref[:, k : k + 1], logits, 0.0),
            axis=1,
            keepdims=True,
        )
        for k in range(TOP)
    ]
    for k in range(TOP):
        gates[k] = jnp.broadcast_to(
            jax.nn.sigmoid(chosen[k] - chosen[1 - k]), (rows, 128)
        )

    load[5].wait()
    load[6].wait()

    def expert(source):
        x = arrived[source]
        for f in range(0, hidden_width, step_cols):
            size = min(step_cols, hidden_width - f)
            gate = jnp.dot(x, w_in[:, f : f + size], preferred_element_type=F32)
            up = jnp.dot(
                x,
                w_in[:, hidden_width + f : hidden_width + f + size],
                preferred_element_type=F32,
            )
            hidden[:, f : f + size] = (jax.nn.gelu(gate, approximate=True) * up).astype(BF16)
        for c in range(0, width, step_cols):
            result[source, :, c : c + step_cols] = jnp.dot(
                hidden[...], w_out[:, c : c + step_cols], preferred_element_type=F32
            ).astype(BF16)

    def serve(d, carry):
        source = xor_index(me_exp, d, n_exp)

        @pl.when(d > 0)
        def _():
            disp_copy(me_exp, source).wait_recv()

        expert(source)

        @pl.when(d > 0)
        def _():
            back_copy(source, me_exp).start()

        return carry

    lax.fori_loop(0, n_exp, serve, 0)

    def combine(exp, rows_of):
        both = jnp.dot(pick[exp], rows_of, preferred_element_type=F32)
        resid[...] += both[:rows] * gates[0, :, 0:1] + both[rows:] * gates[1, :, 0:1]

    combine(me_exp, result[me_exp])

    def take(d, carry):
        exp = xor_index(me_exp, d, n_exp)
        back_copy(me_exp, exp).wait_recv()
        combine(exp, collected[exp])
        return carry

    lax.fori_loop(1, n_exp, take, 0)
    out_ref[...] = rms_scale(resid[...], gain_out_ref[...].astype(F32)).astype(BF16)

    def sent(d, carry):
        other = xor_index(me_exp, d, n_exp)
        disp_copy(other, me_exp).wait_send()
        back_copy(other, me_exp).wait_send()
        return carry

    lax.fori_loop(1, n_exp, sent, 0)

    def pages_sent(s, carry):
        for side in range(2):
            block_z = z - s if side == 0 else z + s
            here = block_z >= 0 if side == 0 else block_z < n_z
            onward = z < n_z - 1 if side == 0 else z > 0
            page = block_z * CORES + core

            @pl.when(here)
            def _():
                for half in range(HALVES):

                    @pl.when(onward)
                    def _():
                        ring_copy(page, half, side).wait_send()

                    pair_copy(page, half).wait_send()

        return carry

    lax.fori_loop(1, n_z, pages_sent, 0)
    for half in range(HALVES):

        @pl.when(z < n_z - 1)
        def _():
            ring_copy(me_req, half, 0, own=True).wait_send()

        @pl.when(z > 0)
        def _():
            ring_copy(me_req, half, 1, own=True).wait_send()

        pair_copy(me_req, half, own=True).wait_send()


def on_device(
    n_exp,
    n_req,
    queries,
    self_kv,
    kv_pages,
    page_table,
    lengths,
    routes,
    residual,
    w_attn_out,
    gain_attn,
    w_router,
    w_in,
    w_out,
    gain_out,
):
    rows, width = residual.shape
    page_len = kv_pages.shape[1]
    hidden_width = w_out.shape[1]
    cap = (5 * rows * TOP + 4 * n_exp - 1) // (4 * n_exp)
    vmem = pl.BlockSpec(memory_space=pltpu.VMEM)
    hbm = pl.BlockSpec(memory_space=pl.ANY)
    dma = pltpu.SemaphoreType.DMA
    return pl.pallas_call(
        functools.partial(layer_kernel, n_exp, n_req),
        out_shape=jax.ShapeDtypeStruct((rows, width), BF16),
        in_specs=[hbm, hbm, hbm, vmem, vmem, vmem, vmem, hbm, hbm, vmem, vmem, hbm, hbm, vmem],
        out_specs=vmem,
        scratch_shapes=[
            pltpu.VMEM((n_req, page_len, 2 * HD), BF16),
            pltpu.VMEM((rows, HD), BF16),
            pltpu.VMEM((rows, 2 * HD), BF16),
            pltpu.VMEM((rows, width), BF16),
            pltpu.VMEM((HD, width), BF16),
            pltpu.VMEM((width, 2 * hidden_width), BF16),
            pltpu.VMEM((hidden_width, width), BF16),
            pltpu.VMEM((rows, CORES * page_len), F32),
            pltpu.VMEM((HEADS, rows, LANES), F32),
            pltpu.VMEM((HEADS, rows, LANES), F32),
            pltpu.VMEM((rows, HD), BF16),
            pltpu.VMEM((rows, width), F32),
            pltpu.VMEM((rows, width), BF16),
            pltpu.VMEM((n_exp, cap, rows), BF16),
            pltpu.VMEM((n_exp, TOP * rows, cap), BF16),
            pltpu.VMEM((TOP, rows, 128), F32),
            pltpu.VMEM((n_exp, cap, width), BF16),
            pltpu.VMEM((n_exp, cap, width), BF16),
            pltpu.VMEM((cap, hidden_width), BF16),
            pltpu.VMEM((n_exp, cap, width), BF16),
            pltpu.VMEM((n_exp, cap, width), BF16),
            dma((7,)),
            dma((2, n_req, HALVES)),
            dma((n_req, HALVES)),
            dma((n_req, HALVES)),
            dma((n_exp,)),
            dma((n_exp,)),
            dma((n_exp,)),
            dma((n_exp,)),
        ],
        compiler_params=pltpu.CompilerParams(
            collective_id=0, has_side_effects=True, vmem_limit_bytes=56 * 2**20
        ),
    )(
        queries,
        self_kv,
        kv_pages,
        page_table,
        lengths.reshape(rows, 1),
        routes,
        routes.T,
        residual,
        w_attn_out,
        gain_attn.reshape(1, width),
        w_router,
        w_in,
        w_out,
        gain_out.reshape(1, width),
    )


def solution(mesh):
    in_specs = (
        P(("expert", "req"), None),
        P(("expert", "req"), None),
        P(("expert", "req"), None, None),
        P("expert", None),
        P(("expert", "req")),
        P(("expert", "req"), None),
        P(("expert", "req"), None),
        P(),
        P(),
        P(),
        P("expert", None, None),
        P("expert", None, None),
        P(),
    )
    out_specs = P(("expert", "req"), None)
    return jax.shard_map(
        functools.partial(on_device, mesh.shape["expert"], mesh.shape["req"]),
        mesh=mesh,
        in_specs=in_specs,
        out_specs=out_specs,
        check_vma=False,
    )
```

```python
import functools
import math

import jax
import jax.numpy as jnp
from jax import lax
from jax.experimental import pallas as pl
from jax.experimental.pallas import tpu as pltpu
from jax.sharding import PartitionSpec as P

HEADS = 16
HEAD_DIM = 64
TOP = 2
PAIRS = HEADS // 2
LANES = 2 * HEAD_DIM
HD = HEADS * HEAD_DIM
CORES = 2
HALVES = 2
NORM_EPS = 1e-06
EXP_SCALE = math.log2(math.e) / math.sqrt(HEAD_DIM)
F32 = jnp.float32
BF16 = jnp.bfloat16


def xor_index(a, b, count):
    out, bit = 0, 1
    while bit < count:
        out = out + ((a // bit + b // bit) % 2) * bit
        bit *= 2
    return out


def rms_scale(values, gain_row):
    mean_square = jnp.mean(values * values, axis=-1, keepdims=True)
    return values * lax.rsqrt(mean_square + NORM_EPS) * gain_row


def gain_row(gain_ref):
    gain = gain_ref[...].astype(F32)
    return jnp.concatenate([gain[i : i + 1, :] for i in range(gain.shape[0])], axis=1)


def layer_kernel(
    n_exp,
    n_req,
    q_hbm,
    self_hbm,
    page_hbm,
    table_ref,
    lengths_t_ref,
    routes_t_ref,
    resid_hbm,
    w_attn_hbm,
    gain_attn_ref,
    w_router_t_ref,
    w_in_hbm,
    w_out_hbm,
    gain_out_ref,
    out_ref,
    kv,
    q,
    self_kv,
    resid_in,
    w_attn,
    w_in,
    w_out,
    bias,
    top,
    acc,
    attended,
    resid,
    normed,
    assign,
    pick,
    gates,
    disp,
    arrived,
    hidden,
    result,
    collected,
    load_sem,
    ring_send,
    pair_send,
    page_recv,
    disp_send,
    disp_recv,
    back_send,
    back_recv,
):
    me_exp = lax.axis_index("expert")
    me_req = lax.axis_index("req")
    z, core = me_req // CORES, me_req % CORES
    n_z = n_req // CORES
    rows = q.shape[0]
    page_len = kv.shape[1]
    half_len = page_len // HALVES
    cap = disp.shape[1]
    hidden_width = w_out.shape[0]
    width = resid.shape[1]
    sibling = z * CORES + (1 - core)

    def at_req(req):
        return {"req": req}

    def at_exp(exp):
        return {"expert": exp}

    loads = [
        (page_hbm.at[0], kv.at[me_req]),
        (q_hbm, q),
        (self_hbm, self_kv),
        (resid_hbm, resid_in),
        (w_attn_hbm, w_attn),
        (w_in_hbm.at[0], w_in),
        (w_out_hbm.at[0], w_out),
    ]
    load = [
        pltpu.make_async_copy(src, dst, load_sem.at[i]) for i, (src, dst) in enumerate(loads)
    ]
    for copy in load:
        copy.start()

    barrier = pltpu.get_barrier_semaphore()

    def greet(device):
        pl.semaphore_signal(
            barrier, inc=1, device_id=device, device_id_type=pl.DeviceIdType.MESH
        )

    greet(at_req(sibling))

    @pl.when(z > 0)
    def _():
        greet(at_req(me_req - CORES))

    @pl.when(z < n_z - 1)
    def _():
        greet(at_req(me_req + CORES))

    for d in range(1, n_exp):
        greet(at_exp(xor_index(me_exp, d, n_exp)))
    pl.semaphore_wait(barrier, n_exp + jnp.where(z > 0, 1, 0) + jnp.where(z < n_z - 1, 1, 0))

    def half_of(page, half):
        return kv.at[page, pl.ds(half * half_len, half_len)]

    def ring_copy(page, half, side, own=False):
        src = page_hbm.at[0, pl.ds(half * half_len, half_len)] if own else half_of(page, half)
        return pltpu.make_async_remote_copy(
            src_ref=src,
            dst_ref=half_of(page, half),
            send_sem=ring_send.at[side, page, half],
            recv_sem=page_recv.at[page, half],
            device_id=at_req(me_req + CORES * (1 - 2 * side)),
            device_id_type=pl.DeviceIdType.MESH,
        )

    def pair_copy(page, half, own=False):
        src = page_hbm.at[0, pl.ds(half * half_len, half_len)] if own else half_of(page, half)
        return pltpu.make_async_remote_copy(
            src_ref=src,
            dst_ref=half_of(page, half),
            send_sem=pair_send.at[page, half],
            recv_sem=page_recv.at[page, half],
            device_id=at_req(sibling),
            device_id_type=pl.DeviceIdType.MESH,
        )

    for half in range(HALVES):

        @pl.when(z < n_z - 1)
        def _():
            ring_copy(me_req, half, 0, own=True).start()

        @pl.when(z > 0)
        def _():
            ring_copy(me_req, half, 1, own=True).start()

    for half in range(HALVES):
        pair_copy(me_req, half, own=True).start()

    diagonal = lax.broadcasted_iota(jnp.int32, (rows, rows), 0) == lax.broadcasted_iota(
        jnp.int32, (rows, rows), 1
    )

    def to_column(row):
        return jnp.sum(jnp.where(diagonal, row, 0), axis=1, keepdims=True)

    lengths = to_column(lengths_t_ref[...])
    routes = [to_column(routes_t_ref[k : k + 1, :]) for k in range(TOP)]
    strict = (
        lax.broadcasted_iota(jnp.int32, (rows, rows), 0)
        > lax.broadcasted_iota(jnp.int32, (rows, rows), 1)
    ).astype(F32).astype(BF16)
    strict_t = (
        lax.broadcasted_iota(jnp.int32, (rows, rows), 0)
        < lax.broadcasted_iota(jnp.int32, (rows, rows), 1)
    ).astype(F32).astype(BF16)
    exp_lane = lax.broadcasted_iota(jnp.int32, (rows, 128), 1)
    exp_row = lax.broadcasted_iota(jnp.int32, (n_exp, rows), 0)
    total = jnp.zeros((1, 128), F32)
    total_t = jnp.zeros((n_exp, 1), F32)
    slots, slots_t = [], []
    for k in range(TOP):
        route = routes[k]
        hot = (exp_lane == route).astype(F32)
        before = jnp.dot(strict, hot.astype(BF16), preferred_element_type=F32) + total
        place = jnp.sum(before * hot, axis=1, keepdims=True).astype(jnp.int32)
        slots.append(jnp.where(place < cap, route * cap + place, -1))
        total = total + jnp.sum(hot, axis=0, keepdims=True)
        route_t = routes_t_ref[k : k + 1, :]
        hot_t = (exp_row == route_t).astype(F32)
        before_t = jnp.dot(hot_t.astype(BF16), strict_t, preferred_element_type=F32) + total_t
        place_t = jnp.sum(before_t * hot_t, axis=0, keepdims=True).astype(jnp.int32)
        slots_t.append(jnp.where(place_t < cap, route_t * cap + place_t, -1))
        total_t = total_t + jnp.sum(hot_t, axis=1, keepdims=True)

    def fill_tables(e, carry):
        slot_row = lax.broadcasted_iota(jnp.int32, (cap, rows), 0) + e * cap
        taken = (slot_row == slots_t[0]).astype(F32) + (slot_row == slots_t[1]).astype(F32)
        assign[e] = taken.astype(BF16)
        slot_lane = lax.broadcasted_iota(jnp.int32, (rows, cap), 1) + e * cap
        for k in range(TOP):
            pick[e, k * rows : (k + 1) * rows, :] = (
                (slot_lane == slots[k]).astype(F32).astype(BF16)
            )
        return carry

    lax.fori_loop(0, n_exp, fill_tables, 0)

    first_lanes = lax.broadcasted_iota(jnp.int32, (1, LANES), 1) < HEAD_DIM

    def own_part(pair, carry):
        lanes = pl.ds(pl.multiple_of(pair * LANES, LANES), LANES)
        product = q[:, lanes].astype(F32) * self_kv[:, lanes].astype(F32)
        own_value = self_kv[
            :, pl.ds(pl.multiple_of(HD + pair * LANES, LANES), LANES)
        ].astype(F32)
        for i in range(2):
            mine = first_lanes if i == 0 else jnp.logical_not(first_lanes)
            score = jnp.sum(jnp.where(mine, product, 0.0), axis=1, keepdims=True)
            top[2 * pair + i] = jnp.broadcast_to(score, (rows, LANES))
            acc[2 * pair + i] = jnp.where(mine, own_value, 1.0)
        return carry

    load[1].wait()
    load[2].wait()
    lax.fori_loop(0, PAIRS, own_part, 0)

    keys = CORES * page_len
    table = table_ref[...]
    logical = lax.broadcasted_iota(jnp.int32, table.shape, 1)

    def attend(block_z):
        key_lane = lax.broadcasted_iota(jnp.int32, (1, keys), 1)
        place = key_lane % page_len
        for c in range(CORES):
            at = jnp.sum(
                jnp.where(table == block_z * CORES + c, logical, 0), axis=1, keepdims=True
            )
            place = place + jnp.where(key_lane // page_len == c, at * page_len, 0)
        bias[...] = jnp.where(place < lengths, 0.0, -jnp.inf)

        def heads(pair, carry):
            lanes = pl.ds(pl.multiple_of(pair * LANES, LANES), LANES)
            value_lanes = pl.ds(pl.multiple_of(HD + pair * LANES, LANES), LANES)
            query = q[:, lanes]
            key = jnp.concatenate(
                [kv[block_z * CORES + c, :, lanes] for c in range(CORES)], axis=0
            )
            value = jnp.concatenate(
                [kv[block_z * CORES + c, :, value_lanes] for c in range(CORES)], axis=0
            )
            for i in range(2):
                mine = first_lanes if i == 0 else jnp.logical_not(first_lanes)
                score = lax.dot_general(
                    jnp.where(mine, query, jnp.zeros_like(query)),
                    key,
                    (((1,), (1,)), ((), ())),
                    preferred_element_type=F32,
                ) + bias[...]
                old = top[2 * pair + i]
                new = jnp.maximum(old, jnp.max(score, axis=1, keepdims=True))
                weight = jnp.exp2(
                    (score - jnp.concatenate([new] * (keys // LANES), axis=1)) * EXP_SCALE
                )
                factor = jnp.exp2((old - new) * EXP_SCALE)
                top[2 * pair + i] = new
                acc[2 * pair + i] = acc[2 * pair + i] * factor + jnp.dot(
                    weight.astype(BF16),
                    jnp.where(mine, value, jnp.ones_like(value)),
                    preferred_element_type=F32,
                )
            return carry

        def heads_two(step, carry):
            heads(2 * step, carry)
            heads(2 * step + 1, carry)
            return carry

        lax.fori_loop(0, PAIRS // 2, heads_two, 0)

    load[0].wait()
    for half in range(HALVES):
        pair_copy(sibling, half).wait_recv()
    attend(z)

    def stage(s, carry):
        for half in range(HALVES):
            for side in range(2):
                block_z = z - s if side == 0 else z + s
                here = block_z >= 0 if side == 0 else block_z < n_z
                onward = z < n_z - 1 if side == 0 else z > 0
                page = block_z * CORES + core

                @pl.when(here)
                def _():
                    ring_copy(page, half, side).wait_recv()

                    @pl.when(onward)
                    def _():
                        ring_copy(page, half, side).start()

                    pair_copy(page, half).start()

            before_z = z - s + 1 if half == 0 else z + s - 1
            before = before_z >= 0 if half == 0 else before_z < n_z

            @pl.when(jnp.logical_and(before, s > 1))
            def _():
                for part in range(HALVES):
                    pair_copy(before_z * CORES + (1 - core), part).wait_recv()
                attend(before_z)

        return carry

    lax.fori_loop(1, n_z + 1, stage, 0)

    for pair in range(PAIRS):
        first, second = acc[2 * pair], acc[2 * pair + 1]
        attended[:, pair * LANES : (pair + 1) * LANES] = jnp.where(
            first_lanes,
            first / first[:, LANES - 1 : LANES],
            second / second[:, 0:1],
        ).astype(BF16)

    load[3].wait()
    load[4].wait()
    step_cols = 256
    for c in range(0, width, step_cols):
        resid[:, c : c + step_cols] = resid_in[:, c : c + step_cols].astype(F32) + jnp.dot(
            attended[...], w_attn[:, c : c + step_cols], preferred_element_type=F32
        )
    normed[...] = rms_scale(resid[...], gain_row(gain_attn_ref)).astype(BF16)

    def disp_copy(exp, source):
        return pltpu.make_async_remote_copy(
            src_ref=disp.at[exp],
            dst_ref=arrived.at[source],
            send_sem=disp_send.at[exp],
            recv_sem=disp_recv.at[source],
            device_id=at_exp(exp),
            device_id_type=pl.DeviceIdType.MESH,
        )

    def back_copy(source, exp):
        return pltpu.make_async_remote_copy(
            src_ref=result.at[source],
            dst_ref=collected.at[exp],
            send_sem=back_send.at[source],
            recv_sem=back_recv.at[exp],
            device_id=at_exp(source),
            device_id_type=pl.DeviceIdType.MESH,
        )

    def gather_slots(exp):
        return jnp.dot(assign[exp], normed[...], preferred_element_type=F32).astype(BF16)

    def send_slots(d, carry):
        exp = xor_index(me_exp, d, n_exp)
        disp[exp] = gather_slots(exp)
        disp_copy(exp, me_exp).start()
        return carry

    lax.fori_loop(1, n_exp, send_slots, 0)
    arrived[me_exp] = gather_slots(me_exp)

    logits = lax.dot_general(
        normed[...],
        w_router_t_ref[...],
        (((1,), (1,)), ((), ())),
        preferred_element_type=F32,
    )
    router_lane = lax.broadcasted_iota(jnp.int32, logits.shape, 1)
    chosen = [
        jnp.sum(
            jnp.where(router_lane == routes[k], logits, 0.0),
            axis=1,
            keepdims=True,
        )
        for k in range(TOP)
    ]
    for k in range(TOP):
        gates[k] = jnp.broadcast_to(
            jax.nn.sigmoid(chosen[k] - chosen[1 - k]), (rows, 128)
        )

    load[5].wait()
    load[6].wait()

    def expert(source):
        x = arrived[source]
        for f in range(0, hidden_width, step_cols):
            size = min(step_cols, hidden_width - f)
            gate = jnp.dot(x, w_in[:, f : f + size], preferred_element_type=F32)
            up = jnp.dot(
                x,
                w_in[:, hidden_width + f : hidden_width + f + size],
                preferred_element_type=F32,
            )
            hidden[:, f : f + size] = (jax.nn.gelu(gate, approximate=True) * up).astype(BF16)
        for c in range(0, width, step_cols):
            result[source, :, c : c + step_cols] = jnp.dot(
                hidden[...], w_out[:, c : c + step_cols], preferred_element_type=F32
            ).astype(BF16)

    def serve(d, carry):
        source = xor_index(me_exp, d, n_exp)

        @pl.when(d > 0)
        def _():
            disp_copy(me_exp, source).wait_recv()

        expert(source)

        @pl.when(d > 0)
        def _():
            back_copy(source, me_exp).start()

        return carry

    lax.fori_loop(0, n_exp, serve, 0)

    def combine(exp, rows_of):
        both = jnp.dot(pick[exp], rows_of, preferred_element_type=F32)
        resid[...] += both[:rows] * gates[0, :, 0:1] + both[rows:] * gates[1, :, 0:1]

    combine(me_exp, result[me_exp])

    def take(d, carry):
        exp = xor_index(me_exp, d, n_exp)
        back_copy(me_exp, exp).wait_recv()
        combine(exp, collected[exp])
        return carry

    lax.fori_loop(1, n_exp, take, 0)
    out_ref[...] = rms_scale(resid[...], gain_row(gain_out_ref)).astype(BF16)

    def sent(d, carry):
        other = xor_index(me_exp, d, n_exp)
        disp_copy(other, me_exp).wait_send()
        back_copy(other, me_exp).wait_send()
        return carry

    lax.fori_loop(1, n_exp, sent, 0)

    def pages_sent(s, carry):
        for side in range(2):
            block_z = z - s if side == 0 else z + s
            here = block_z >= 0 if side == 0 else block_z < n_z
            onward = z < n_z - 1 if side == 0 else z > 0
            page = block_z * CORES + core

            @pl.when(here)
            def _():
                for half in range(HALVES):

                    @pl.when(onward)
                    def _():
                        ring_copy(page, half, side).wait_send()

                    pair_copy(page, half).wait_send()

        return carry

    lax.fori_loop(1, n_z, pages_sent, 0)
    for half in range(HALVES):

        @pl.when(z < n_z - 1)
        def _():
            ring_copy(me_req, half, 0, own=True).wait_send()

        @pl.when(z > 0)
        def _():
            ring_copy(me_req, half, 1, own=True).wait_send()

        pair_copy(me_req, half, own=True).wait_send()


def on_device(
    n_exp,
    n_req,
    queries,
    self_kv,
    kv_pages,
    page_table,
    lengths,
    routes,
    residual,
    w_attn_out,
    gain_attn,
    w_router,
    w_in,
    w_out,
    gain_out,
):
    rows, width = residual.shape
    page_len = kv_pages.shape[1]
    hidden_width = w_out.shape[1]
    cap = (5 * rows * TOP + 4 * n_exp - 1) // (4 * n_exp)
    vmem = pl.BlockSpec(memory_space=pltpu.VMEM)
    hbm = pl.BlockSpec(memory_space=pl.ANY)
    dma = pltpu.SemaphoreType.DMA
    return pl.pallas_call(
        functools.partial(layer_kernel, n_exp, n_req),
        out_shape=jax.ShapeDtypeStruct((rows, width), BF16),
        in_specs=[hbm, hbm, hbm, vmem, vmem, vmem, hbm, hbm, vmem, vmem, hbm, hbm, vmem],
        out_specs=vmem,
        scratch_shapes=[
            pltpu.VMEM((n_req, page_len, 2 * HD), BF16),
            pltpu.VMEM((rows, HD), BF16),
            pltpu.VMEM((rows, 2 * HD), BF16),
            pltpu.VMEM((rows, width), BF16),
            pltpu.VMEM((HD, width), BF16),
            pltpu.VMEM((width, 2 * hidden_width), BF16),
            pltpu.VMEM((hidden_width, width), BF16),
            pltpu.VMEM((rows, CORES * page_len), F32),
            pltpu.VMEM((HEADS, rows, LANES), F32),
            pltpu.VMEM((HEADS, rows, LANES), F32),
            pltpu.VMEM((rows, HD), BF16),
            pltpu.VMEM((rows, width), F32),
            pltpu.VMEM((rows, width), BF16),
            pltpu.VMEM((n_exp, cap, rows), BF16),
            pltpu.VMEM((n_exp, TOP * rows, cap), BF16),
            pltpu.VMEM((TOP, rows, 128), F32),
            pltpu.VMEM((n_exp, cap, width), BF16),
            pltpu.VMEM((n_exp, cap, width), BF16),
            pltpu.VMEM((cap, hidden_width), BF16),
            pltpu.VMEM((n_exp, cap, width), BF16),
            pltpu.VMEM((n_exp, cap, width), BF16),
            dma((7,)),
            dma((2, n_req, HALVES)),
            dma((n_req, HALVES)),
            dma((n_req, HALVES)),
            dma((n_exp,)),
            dma((n_exp,)),
            dma((n_exp,)),
            dma((n_exp,)),
        ],
        compiler_params=pltpu.CompilerParams(
            collective_id=0, has_side_effects=True, vmem_limit_bytes=56 * 2**20
        ),
    )(
        queries,
        self_kv,
        kv_pages,
        page_table,
        lengths.reshape(1, rows),
        routes.T,
        residual,
        w_attn_out,
        gain_attn.reshape(width // 128, 128),
        w_router.T,
        w_in,
        w_out,
        gain_out.reshape(width // 128, 128),
    )


def solution(mesh):
    in_specs = (
        P(("expert", "req"), None),
        P(("expert", "req"), None),
        P(("expert", "req"), None, None),
        P("expert", None),
        P(("expert", "req")),
        P(("expert", "req"), None),
        P(("expert", "req"), None),
        P(),
        P(),
        P(),
        P("expert", None, None),
        P("expert", None, None),
        P(),
    )
    out_specs = P(("expert", "req"), None)
    return jax.shard_map(
        functools.partial(on_device, mesh.shape["expert"], mesh.shape["req"]),
        mesh=mesh,
        in_specs=in_specs,
        out_specs=out_specs,
        check_vma=False,
    )
```

```python
import functools
import math

import jax
import jax.numpy as jnp
from jax import lax
from jax.experimental import pallas as pl
from jax.experimental.pallas import tpu as pltpu
from jax.sharding import PartitionSpec as P

HEADS = 16
HEAD_DIM = 64
TOP = 2
PAIRS = HEADS // 2
LANES = 2 * HEAD_DIM
HD = HEADS * HEAD_DIM
CORES = 2
HALVES = 2
NORM_EPS = 1e-06
EXP_SCALE = math.log2(math.e) / math.sqrt(HEAD_DIM)
F32 = jnp.float32
BF16 = jnp.bfloat16


def xor_index(a, b, count):
    out, bit = 0, 1
    while bit < count:
        out = out + ((a // bit + b // bit) % 2) * bit
        bit *= 2
    return out


def rms_scale(values, gain_row):
    mean_square = jnp.mean(values * values, axis=-1, keepdims=True)
    return values * lax.rsqrt(mean_square + NORM_EPS) * gain_row


def gain_row(gain_ref):
    gain = gain_ref[...].astype(F32)
    return jnp.concatenate([gain[i : i + 1, :] for i in range(gain.shape[0])], axis=1)


def layer_kernel(
    n_exp,
    n_req,
    q_hbm,
    self_hbm,
    page_hbm,
    table_ref,
    lengths_t_ref,
    routes_t_ref,
    resid_hbm,
    w_attn_hbm,
    gain_attn_ref,
    w_router_t_ref,
    w_in_hbm,
    w_out_hbm,
    gain_out_ref,
    out_ref,
    kv,
    q,
    self_kv,
    resid_in,
    w_attn,
    w_in,
    w_out,
    bias,
    top,
    acc,
    attended,
    resid,
    normed,
    assign,
    pick,
    gates,
    disp,
    arrived,
    hidden,
    result,
    collected,
    load_sem,
    ring_send,
    pair_send,
    page_recv,
    disp_send,
    disp_recv,
    back_send,
    back_recv,
):
    me_exp = lax.axis_index("expert")
    me_req = lax.axis_index("req")
    z, core = me_req // CORES, me_req % CORES
    n_z = n_req // CORES
    rows = q.shape[0]
    page_len = kv.shape[1]
    half_len = page_len // HALVES
    cap = disp.shape[1]
    hidden_width = w_out.shape[0]
    width = resid.shape[1]
    sibling = z * CORES + (1 - core)

    def at_req(req):
        return {"req": req}

    def at_exp(exp):
        return {"expert": exp}

    loads = [
        (page_hbm.at[0], kv.at[me_req]),
        (q_hbm, q),
        (self_hbm, self_kv),
        (resid_hbm, resid_in),
        (w_attn_hbm, w_attn),
        (w_in_hbm.at[0], w_in),
        (w_out_hbm.at[0], w_out),
    ]
    load = [
        pltpu.make_async_copy(src, dst, load_sem.at[i]) for i, (src, dst) in enumerate(loads)
    ]
    for copy in load:
        copy.start()

    barrier = pltpu.get_barrier_semaphore()

    def greet(device):
        pl.semaphore_signal(
            barrier, inc=1, device_id=device, device_id_type=pl.DeviceIdType.MESH
        )

    greet(at_req(sibling))

    @pl.when(z > 0)
    def _():
        greet(at_req(me_req - CORES))

    @pl.when(z < n_z - 1)
    def _():
        greet(at_req(me_req + CORES))

    for d in range(1, n_exp):
        greet(at_exp(xor_index(me_exp, d, n_exp)))
    pl.semaphore_wait(barrier, n_exp + jnp.where(z > 0, 1, 0) + jnp.where(z < n_z - 1, 1, 0))

    def half_of(page, half):
        return kv.at[page, pl.ds(pl.multiple_of(half * half_len, half_len), half_len)]

    def ring_copy(page, half, side, own=False):
        src = page_hbm.at[0, pl.ds(half * half_len, half_len)] if own else half_of(page, half)
        return pltpu.make_async_remote_copy(
            src_ref=src,
            dst_ref=half_of(page, half),
            send_sem=ring_send.at[side, page, half],
            recv_sem=page_recv.at[page, half],
            device_id=at_req(me_req + CORES * (1 - 2 * side)),
            device_id_type=pl.DeviceIdType.MESH,
        )

    def pair_copy(page, half, own=False):
        src = page_hbm.at[0, pl.ds(half * half_len, half_len)] if own else half_of(page, half)
        return pltpu.make_async_remote_copy(
            src_ref=src,
            dst_ref=half_of(page, half),
            send_sem=pair_send.at[page, half],
            recv_sem=page_recv.at[page, half],
            device_id=at_req(sibling),
            device_id_type=pl.DeviceIdType.MESH,
        )

    for half in range(HALVES):

        @pl.when(z < n_z - 1)
        def _():
            ring_copy(me_req, half, 0, own=True).start()

        @pl.when(z > 0)
        def _():
            ring_copy(me_req, half, 1, own=True).start()

    for half in range(HALVES):
        pair_copy(me_req, half, own=True).start()

    diagonal = lax.broadcasted_iota(jnp.int32, (rows, rows), 0) == lax.broadcasted_iota(
        jnp.int32, (rows, rows), 1
    )

    def to_column(row):
        return jnp.sum(jnp.where(diagonal, row, 0), axis=1, keepdims=True)

    lengths = to_column(lengths_t_ref[...])
    routes = [to_column(routes_t_ref[k : k + 1, :]) for k in range(TOP)]
    strict = (
        lax.broadcasted_iota(jnp.int32, (rows, rows), 0)
        > lax.broadcasted_iota(jnp.int32, (rows, rows), 1)
    ).astype(F32).astype(BF16)
    strict_t = (
        lax.broadcasted_iota(jnp.int32, (rows, rows), 0)
        < lax.broadcasted_iota(jnp.int32, (rows, rows), 1)
    ).astype(F32).astype(BF16)
    exp_lane = lax.broadcasted_iota(jnp.int32, (rows, 128), 1)
    exp_row = lax.broadcasted_iota(jnp.int32, (n_exp, rows), 0)
    total = jnp.zeros((1, 128), F32)
    total_t = jnp.zeros((n_exp, 1), F32)
    slots, slots_t = [], []
    for k in range(TOP):
        route = routes[k]
        hot = (exp_lane == route).astype(F32)
        before = jnp.dot(strict, hot.astype(BF16), preferred_element_type=F32) + total
        place = jnp.sum(before * hot, axis=1, keepdims=True).astype(jnp.int32)
        slots.append(jnp.where(place < cap, route * cap + place, -1))
        total = total + jnp.sum(hot, axis=0, keepdims=True)
        route_t = routes_t_ref[k : k + 1, :]
        hot_t = (exp_row == route_t).astype(F32)
        before_t = jnp.dot(hot_t.astype(BF16), strict_t, preferred_element_type=F32) + total_t
        place_t = jnp.sum(before_t * hot_t, axis=0, keepdims=True).astype(jnp.int32)
        slots_t.append(jnp.where(place_t < cap, route_t * cap + place_t, -1))
        total_t = total_t + jnp.sum(hot_t, axis=1, keepdims=True)

    def fill_tables(e, carry):
        slot_row = lax.broadcasted_iota(jnp.int32, (cap, rows), 0) + e * cap
        taken = (slot_row == slots_t[0]).astype(F32) + (slot_row == slots_t[1]).astype(F32)
        assign[e] = taken.astype(BF16)
        slot_lane = lax.broadcasted_iota(jnp.int32, (rows, cap), 1) + e * cap
        for k in range(TOP):
            pick[e, k * rows : (k + 1) * rows, :] = (
                (slot_lane == slots[k]).astype(F32).astype(BF16)
            )
        return carry

    lax.fori_loop(0, n_exp, fill_tables, 0)

    first_lanes = lax.broadcasted_iota(jnp.int32, (1, LANES), 1) < HEAD_DIM

    def own_part(pair, carry):
        lanes = pl.ds(pl.multiple_of(pair * LANES, LANES), LANES)
        product = q[:, lanes].astype(F32) * self_kv[:, lanes].astype(F32)
        own_value = self_kv[
            :, pl.ds(pl.multiple_of(HD + pair * LANES, LANES), LANES)
        ].astype(F32)
        for i in range(2):
            mine = first_lanes if i == 0 else jnp.logical_not(first_lanes)
            score = jnp.sum(jnp.where(mine, product, 0.0), axis=1, keepdims=True)
            top[2 * pair + i] = jnp.broadcast_to(score, (rows, LANES))
            acc[2 * pair + i] = jnp.where(mine, own_value, 1.0)
        return carry

    load[1].wait()
    load[2].wait()
    lax.fori_loop(0, PAIRS, own_part, 0)

    keys = CORES * half_len
    table = table_ref[...]
    logical = lax.broadcasted_iota(jnp.int32, table.shape, 1)

    def attend(block_z, half):
        span = pl.ds(pl.multiple_of(half * half_len, half_len), half_len)
        key_lane = lax.broadcasted_iota(jnp.int32, (1, keys), 1)
        place = key_lane % half_len + half * half_len
        for c in range(CORES):
            at = jnp.sum(
                jnp.where(table == block_z * CORES + c, logical, 0), axis=1, keepdims=True
            )
            place = place + jnp.where(key_lane // half_len == c, at * page_len, 0)
        bias[...] = jnp.where(place < lengths, 0.0, -jnp.inf)

        def heads(pair, carry):
            lanes = pl.ds(pl.multiple_of(pair * LANES, LANES), LANES)
            value_lanes = pl.ds(pl.multiple_of(HD + pair * LANES, LANES), LANES)
            query = q[:, lanes]
            key = jnp.concatenate(
                [kv[block_z * CORES + c, span, lanes] for c in range(CORES)], axis=0
            )
            value = jnp.concatenate(
                [kv[block_z * CORES + c, span, value_lanes] for c in range(CORES)], axis=0
            )
            for i in range(2):
                mine = first_lanes if i == 0 else jnp.logical_not(first_lanes)
                score = lax.dot_general(
                    jnp.where(mine, query, jnp.zeros_like(query)),
                    key,
                    (((1,), (1,)), ((), ())),
                    preferred_element_type=F32,
                ) + bias[...]
                old = top[2 * pair + i]
                new = jnp.maximum(old, jnp.max(score, axis=1, keepdims=True))
                weight = jnp.exp2(
                    (score - jnp.concatenate([new] * (keys // LANES), axis=1)) * EXP_SCALE
                )
                factor = jnp.exp2((old - new) * EXP_SCALE)
                top[2 * pair + i] = new
                acc[2 * pair + i] = acc[2 * pair + i] * factor + jnp.dot(
                    weight.astype(BF16),
                    jnp.where(mine, value, jnp.ones_like(value)),
                    preferred_element_type=F32,
                )
            return carry

        def heads_two(step, carry):
            heads(2 * step, carry)
            heads(2 * step + 1, carry)
            return carry

        lax.fori_loop(0, PAIRS // 2, heads_two, 0)

    load[0].wait()
    for half in range(HALVES):
        pair_copy(sibling, half).wait_recv()
        attend(z, half)

    def stage(t, carry):
        s, half = t // HALVES + 1, t % HALVES
        for side in range(2):
            block_z = z - s if side == 0 else z + s
            here = block_z >= 0 if side == 0 else block_z < n_z
            onward = z < n_z - 1 if side == 0 else z > 0
            page = block_z * CORES + core

            @pl.when(here)
            def _():
                ring_copy(page, half, side).wait_recv()

                @pl.when(onward)
                def _():
                    ring_copy(page, half, side).start()

                pair_copy(page, half).start()

        for side in range(2):
            block_z = z - s if side == 0 else z + s
            here = block_z >= 0 if side == 0 else block_z < n_z

            @pl.when(here)
            def _():
                pair_copy(block_z * CORES + (1 - core), half).wait_recv()
                attend(block_z, half)

        return carry

    lax.fori_loop(0, HALVES * (n_z - 1), stage, 0)

    for pair in range(PAIRS):
        first, second = acc[2 * pair], acc[2 * pair + 1]
        attended[:, pair * LANES : (pair + 1) * LANES] = jnp.where(
            first_lanes,
            first / first[:, LANES - 1 : LANES],
            second / second[:, 0:1],
        ).astype(BF16)

    load[3].wait()
    load[4].wait()
    step_cols = 256
    for c in range(0, width, step_cols):
        resid[:, c : c + step_cols] = resid_in[:, c : c + step_cols].astype(F32) + jnp.dot(
            attended[...], w_attn[:, c : c + step_cols], preferred_element_type=F32
        )
    normed[...] = rms_scale(resid[...], gain_row(gain_attn_ref)).astype(BF16)

    def disp_copy(exp, source):
        return pltpu.make_async_remote_copy(
            src_ref=disp.at[exp],
            dst_ref=arrived.at[source],
            send_sem=disp_send.at[exp],
            recv_sem=disp_recv.at[source],
            device_id=at_exp(exp),
            device_id_type=pl.DeviceIdType.MESH,
        )

    def back_copy(source, exp):
        return pltpu.make_async_remote_copy(
            src_ref=result.at[source],
            dst_ref=collected.at[exp],
            send_sem=back_send.at[source],
            recv_sem=back_recv.at[exp],
            device_id=at_exp(source),
            device_id_type=pl.DeviceIdType.MESH,
        )

    def gather_slots(exp):
        return jnp.dot(assign[exp], normed[...], preferred_element_type=F32).astype(BF16)

    def send_slots(d, carry):
        exp = xor_index(me_exp, d, n_exp)
        disp[exp] = gather_slots(exp)
        disp_copy(exp, me_exp).start()
        return carry

    lax.fori_loop(1, n_exp, send_slots, 0)
    arrived[me_exp] = gather_slots(me_exp)

    logits = lax.dot_general(
        normed[...],
        w_router_t_ref[...],
        (((1,), (1,)), ((), ())),
        preferred_element_type=F32,
    )
    router_lane = lax.broadcasted_iota(jnp.int32, logits.shape, 1)
    chosen = [
        jnp.sum(
            jnp.where(router_lane == routes[k], logits, 0.0),
            axis=1,
            keepdims=True,
        )
        for k in range(TOP)
    ]
    for k in range(TOP):
        gates[k] = jnp.broadcast_to(
            jax.nn.sigmoid(chosen[k] - chosen[1 - k]), (rows, 128)
        )

    load[5].wait()
    load[6].wait()

    def expert(source):
        x = arrived[source]
        for f in range(0, hidden_width, step_cols):
            size = min(step_cols, hidden_width - f)
            gate = jnp.dot(x, w_in[:, f : f + size], preferred_element_type=F32)
            up = jnp.dot(
                x,
                w_in[:, hidden_width + f : hidden_width + f + size],
                preferred_element_type=F32,
            )
            hidden[:, f : f + size] = (jax.nn.gelu(gate, approximate=True) * up).astype(BF16)
        for c in range(0, width, step_cols):
            result[source, :, c : c + step_cols] = jnp.dot(
                hidden[...], w_out[:, c : c + step_cols], preferred_element_type=F32
            ).astype(BF16)

    def serve(d, carry):
        source = xor_index(me_exp, d, n_exp)

        @pl.when(d > 0)
        def _():
            disp_copy(me_exp, source).wait_recv()

        expert(source)

        @pl.when(d > 0)
        def _():
            back_copy(source, me_exp).start()

        return carry

    lax.fori_loop(0, n_exp, serve, 0)

    def combine(exp, rows_of):
        both = jnp.dot(pick[exp], rows_of, preferred_element_type=F32)
        resid[...] += both[:rows] * gates[0, :, 0:1] + both[rows:] * gates[1, :, 0:1]

    combine(me_exp, result[me_exp])

    def take(d, carry):
        exp = xor_index(me_exp, d, n_exp)
        back_copy(me_exp, exp).wait_recv()
        combine(exp, collected[exp])
        return carry

    lax.fori_loop(1, n_exp, take, 0)
    out_ref[...] = rms_scale(resid[...], gain_row(gain_out_ref)).astype(BF16)

    def sent(d, carry):
        other = xor_index(me_exp, d, n_exp)
        disp_copy(other, me_exp).wait_send()
        back_copy(other, me_exp).wait_send()
        return carry

    lax.fori_loop(1, n_exp, sent, 0)

    def pages_sent(s, carry):
        for side in range(2):
            block_z = z - s if side == 0 else z + s
            here = block_z >= 0 if side == 0 else block_z < n_z
            onward = z < n_z - 1 if side == 0 else z > 0
            page = block_z * CORES + core

            @pl.when(here)
            def _():
                for half in range(HALVES):

                    @pl.when(onward)
                    def _():
                        ring_copy(page, half, side).wait_send()

                    pair_copy(page, half).wait_send()

        return carry

    lax.fori_loop(1, n_z, pages_sent, 0)
    for half in range(HALVES):

        @pl.when(z < n_z - 1)
        def _():
            ring_copy(me_req, half, 0, own=True).wait_send()

        @pl.when(z > 0)
        def _():
            ring_copy(me_req, half, 1, own=True).wait_send()

        pair_copy(me_req, half, own=True).wait_send()


def on_device(
    n_exp,
    n_req,
    queries,
    self_kv,
    kv_pages,
    page_table,
    lengths,
    routes,
    residual,
    w_attn_out,
    gain_attn,
    w_router,
    w_in,
    w_out,
    gain_out,
):
    rows, width = residual.shape
    page_len = kv_pages.shape[1]
    hidden_width = w_out.shape[1]
    cap = (5 * rows * TOP + 4 * n_exp - 1) // (4 * n_exp)
    vmem = pl.BlockSpec(memory_space=pltpu.VMEM)
    hbm = pl.BlockSpec(memory_space=pl.ANY)
    dma = pltpu.SemaphoreType.DMA
    return pl.pallas_call(
        functools.partial(layer_kernel, n_exp, n_req),
        out_shape=jax.ShapeDtypeStruct((rows, width), BF16),
        in_specs=[hbm, hbm, hbm, vmem, vmem, vmem, hbm, hbm, vmem, vmem, hbm, hbm, vmem],
        out_specs=vmem,
        scratch_shapes=[
            pltpu.VMEM((n_req, page_len, 2 * HD), BF16),
            pltpu.VMEM((rows, HD), BF16),
            pltpu.VMEM((rows, 2 * HD), BF16),
            pltpu.VMEM((rows, width), BF16),
            pltpu.VMEM((HD, width), BF16),
            pltpu.VMEM((width, 2 * hidden_width), BF16),
            pltpu.VMEM((hidden_width, width), BF16),
            pltpu.VMEM((rows, CORES * page_len // HALVES), F32),
            pltpu.VMEM((HEADS, rows, LANES), F32),
            pltpu.VMEM((HEADS, rows, LANES), F32),
            pltpu.VMEM((rows, HD), BF16),
            pltpu.VMEM((rows, width), F32),
            pltpu.VMEM((rows, width), BF16),
            pltpu.VMEM((n_exp, cap, rows), BF16),
            pltpu.VMEM((n_exp, TOP * rows, cap), BF16),
            pltpu.VMEM((TOP, rows, 128), F32),
            pltpu.VMEM((n_exp, cap, width), BF16),
            pltpu.VMEM((n_exp, cap, width), BF16),
            pltpu.VMEM((cap, hidden_width), BF16),
            pltpu.VMEM((n_exp, cap, width), BF16),
            pltpu.VMEM((n_exp, cap, width), BF16),
            dma((7,)),
            dma((2, n_req, HALVES)),
            dma((n_req, HALVES)),
            dma((n_req, HALVES)),
            dma((n_exp,)),
            dma((n_exp,)),
            dma((n_exp,)),
            dma((n_exp,)),
        ],
        compiler_params=pltpu.CompilerParams(
            collective_id=0, has_side_effects=True, vmem_limit_bytes=56 * 2**20
        ),
    )(
        queries,
        self_kv,
        kv_pages,
        page_table,
        lengths.reshape(1, rows),
        routes.T,
        residual,
        w_attn_out,
        gain_attn.reshape(width // 128, 128),
        w_router.T,
        w_in,
        w_out,
        gain_out.reshape(width // 128, 128),
    )


def solution(mesh):
    in_specs = (
        P(("expert", "req"), None),
        P(("expert", "req"), None),
        P(("expert", "req"), None, None),
        P("expert", None),
        P(("expert", "req")),
        P(("expert", "req"), None),
        P(("expert", "req"), None),
        P(),
        P(),
        P(),
        P("expert", None, None),
        P("expert", None, None),
        P(),
    )
    out_specs = P(("expert", "req"), None)
    return jax.shard_map(
        functools.partial(on_device, mesh.shape["expert"], mesh.shape["req"]),
        mesh=mesh,
        in_specs=in_specs,
        out_specs=out_specs,
        check_vma=False,
    )
```
